256 devices in a mesh: front: 16 (over z, core), tile: 16 (over y, x).
Axes of the slice: x: 4, y: 4, z: 8, core: 2. Of those that a mesh axis runs over, the one named last changes fastest.
Arguments:
- parent_solution: bfloat16 [16, 64, 256, 512], P('tile', 'front'), may hold values from -6 to 6
- segment_ids: int32 [16, 16, 16], P('tile'), may hold values from 0 to 63, as said below
- segment_counts: int32 [16, 16, 2], P('tile'), may hold values from 4 to 8
- row_bases: bfloat16 [16, 16, 2, 8, 16, 64, 256], P('tile', 'front'), may hold values from -0.03125 to 0.03125
- column_bases: bfloat16 [16, 2, 16, 64, 256], P('front', None, 'tile'), may hold values from -0.75 to 0.75
- diag_inverse: bfloat16 [16, 2, 16, 256, 256], P('front', None, 'tile'), may hold values from -0.375 to 0.375
- child_right: bfloat16 [16, 2, 16, 256, 512], P('front', None, 'tile'), may hold values from -6 to 6
- tile_ranks: int32 [16, 2, 16], P('front', None, 'tile'), may hold values from 8 to 64
Outputs:
- child_solution: bfloat16 [16, 2, 16, 256, 512], P('front', None, 'tile')
The draws below stay inside these ranges and needn't reach their ends.
Inputs may be any that keep to these rules, and one draw needn't show every extreme that they name: `segment_ids`: block id // 4 is the front index holding the block. In every row of 16 ids no front index holds more than 2 of the named blocks, and one holds exactly 2.
All inputs are finite; a program needn't handle non-finite values.
Results may differ from the reference program's by a relative error of at most 0.0052.
Values may be sent and summed in bfloat16 or wider, within the bound.
A program may use at most 128 MiB of HBM per device.

```python
import jax
import jax.numpy as jnp
from jax import lax

BLOCK = 256
RANK = 64
RHS = 512
SEG = 8
FRONTS = 2
OWNED = 4
CAP = 2
SLOTS = 16
CBLK = 16
PARENTS = 64
N_FRONT = 16
N_TILE = 16


def forced_top(key, shape, lowest, highest):
    first_key, second_key = jax.random.split(key)
    values = jax.random.randint(first_key, shape, lowest, highest + 1).reshape(-1)
    where_top = jax.random.randint(second_key, (), 0, values.shape[0])
    values = values.at[where_top].set(highest)
    return values.reshape(shape).astype(jnp.int32)


def draw_segment_counts(key, part):
    key = jax.random.fold_in(key, 11)
    return forced_top(key, (N_TILE, N_FRONT, FRONTS), SEG // 2, SEG)


def draw_tile_ranks(key, part):
    key = jax.random.fold_in(key, 12)
    return forced_top(key, (N_FRONT, FRONTS, CBLK), RANK // 8, RANK)


def one_row(key):
    owner_key, local_key = jax.random.split(key)
    owners = jax.random.permutation(owner_key, CAP * N_FRONT)[:SLOTS] // CAP
    first = owners[0]
    first_count = jnp.sum((owners == first).astype(jnp.int32))
    owners = owners.at[SEG].set(jnp.where(first_count == 1, first, owners[SEG]))
    locals_drawn = jax.random.randint(local_key, (SLOTS,), 0, OWNED)
    return (owners * OWNED + locals_drawn).astype(jnp.int32)


def draw_segment_ids(key, part):
    key = jax.random.fold_in(key, 13)
    row_keys = jax.random.split(key, N_TILE * N_FRONT)
    rows_drawn = jax.vmap(one_row)(row_keys)
    return rows_drawn.reshape(N_TILE, N_FRONT, SLOTS)


def level_of(own_key, dims, cuts, smallest, high):
    level, own = 1.0, jax.random.fold_in(own_key, 6)
    for position, blocks in cuts:
        draws = jnp.exp(jax.random.uniform(jax.random.fold_in(own, position), (blocks,), jnp.float32, smallest / len(cuts), high / len(cuts)))
        level = level * jnp.repeat(draws, dims[position] // blocks).reshape([-1 if axis == position else 1 for axis in range(len(dims))])
    return level


def scatter_about(stream_key, dims, deviation, reach, shards=(), held_as=jnp.bfloat16):
    entries = deviation * jax.random.normal(stream_key, dims, jnp.float32)
    if shards:
        entries = entries * level_of(stream_key, dims, shards, -0.22, 0.18)
    return jnp.clip(entries, -reach, reach).astype(held_as)


def setup_inputs(seed: int = 0) -> dict:
    key_of = jax.random.split(jax.random.key(seed), 9)
    parent_solution = scatter_about(key_of[0], (N_TILE, PARENTS, BLOCK, RHS), 1.0, 6.0, ((0, 16), (1, 16)))
    segment_ids = draw_segment_ids(jax.random.fold_in(key_of[8], 71), 0)
    segment_counts = draw_segment_counts(jax.random.fold_in(key_of[8], 71), 0)
    row_bases = scatter_about(key_of[3], (N_TILE, N_FRONT, FRONTS, SEG, CBLK, RANK, BLOCK), (N_TILE * SEG * BLOCK) ** -0.5, 0.03125, ((0, 16), (1, 16)))
    column_bases = scatter_about(key_of[4], (N_FRONT, FRONTS, CBLK, RANK, BLOCK), RANK ** -0.5, 0.75, ((0, 16), (2, 16)))
    diag_inverse = scatter_about(key_of[5], (N_FRONT, FRONTS, CBLK, BLOCK, BLOCK), BLOCK ** -0.5, 0.375, ((0, 16), (2, 16)))
    child_right = scatter_about(key_of[6], (N_FRONT, FRONTS, CBLK, BLOCK, RHS), 1.0, 6.0, ((0, 16), (2, 16)))
    tile_ranks = draw_tile_ranks(jax.random.fold_in(key_of[8], 71), 0)
    return dict(parent_solution=parent_solution, segment_ids=segment_ids, segment_counts=segment_counts, row_bases=row_bases, column_bases=column_bases, diag_inverse=diag_inverse, child_right=child_right, tile_ranks=tile_ranks)


def reference(parent_solution, segment_ids, segment_counts, row_bases, column_bases, diag_inverse, child_right, tile_ranks):
    slot_index = jnp.arange(SLOTS)
    front_of = slot_index // SEG

    def lane_term(summed, lane):
        lane_ids = segment_ids[lane]
        usable = (slot_index % SEG)[None, :] < segment_counts[lane][:, front_of]
        lane_blocks = parent_solution[lane]

        def one_front(front):
            picked = lane_blocks[lane_ids[front]].astype(jnp.float32)
            picked = picked * usable[front].astype(jnp.float32)[:, None, None]
            picked = picked.reshape(FRONTS, SEG, BLOCK, RHS)
            bases = row_bases[lane, front].astype(jnp.float32)
            return jnp.einsum('csjkb,csbr->cjkr', bases, picked)

        return summed + lax.map(one_front, jnp.arange(N_FRONT)), None

    start = jnp.zeros((N_FRONT, FRONTS, CBLK, RANK, RHS), jnp.float32)
    rank_partial, _ = lax.scan(lane_term, start, jnp.arange(N_TILE))
    keep = jnp.arange(RANK)[None, None, None, :, None] < tile_ranks[:, :, :, None, None]
    rank_space = (rank_partial * keep.astype(jnp.float32)).astype(jnp.bfloat16)
    projected = jnp.einsum('fcjkb,fcjkr->fcjbr', column_bases.astype(jnp.float32), rank_space.astype(jnp.float32))
    reduced = (child_right.astype(jnp.float32) - projected).astype(jnp.bfloat16)
    solved = jnp.einsum('fcjab,fcjbr->fcjar', diag_inverse.astype(jnp.float32), reduced.astype(jnp.float32))
    return solved.astype(jnp.bfloat16)
```

```python
import functools

import jax
import jax.numpy as jnp
from jax import lax
from jax.experimental import pallas as pl
from jax.experimental.pallas import tpu as pltpu
from jax.sharding import PartitionSpec as P

MESH = pl.DeviceIdType.MESH

NZ = 8
NY = 4
NX = 4
NT = NY * NX
OWNED = 4
BLOCK = 256
RANK = 64
RHS = 512
SEG = 8
FRONTS = 2
WIDTH = 128
CHUNKS = RHS // WIDTH
NBLK = NZ * 2 * OWNED
GROUP = NX * RANK
PIECES = ((1, 0), (1, 1), (2, 0), (2, 1), (3, 0), (3, 1), (4, 0))
NP = len(PIECES)


def kernel(
    ids, counts, ranks, parent, bases, cols, diag, right_side, out,
    b0, b1, b2, b3, bases_v, cols_v, diag_v, right_v, out_v, part, arrived,
    ring_send, ring_recv, pair_send, pair_recv, tile_send, tile_recv, load_sem, own_sem, out_sem,
):
    blocks = (b0, b1, b2, b3)
    front = lax.axis_index("front")
    tile = lax.axis_index("tile")
    z, core = front // 2, front % 2
    y, x = tile // NX, tile % NX
    sibling = z * 2 + (1 - core)
    ahead = ((z + 1) % NZ) * 2 + core
    behind = ((z + NZ - 1) % NZ) * 2 + core

    def peer(k):
        return ((y + k // NX) % NY) * NX + (x + k % NX) % NX

    barrier = pltpu.get_barrier_semaphore()
    for other in (ahead, behind, sibling):
        pl.semaphore_signal(barrier, inc=1, device_id={"front": other}, device_id_type=MESH)
    for k in range(1, NT):
        pl.semaphore_signal(barrier, inc=1, device_id={"tile": peer(k)}, device_id_type=MESH)
    pl.semaphore_wait(barrier, 3 + NT - 1)

    def place(chip, who, half):
        return pl.ds((chip * 2 + who) * OWNED + half * 2, 2)

    def chunk_cols(r):
        return pl.ds(r * WIDTH, WIDTH)

    def ring(r, i, way):
        hop, half = PIECES[i]
        half = half if way == 0 else 1 - half
        chip = (z + NZ - (hop - 1)) % NZ if way == 0 else (z + hop - 1) % NZ
        dst = blocks[r].at[place(chip, core, half)]
        if hop == 1:
            src = parent.at[pl.ds(half * 2, 2), :, chunk_cols(r)]
        else:
            src = dst
        return pltpu.make_async_remote_copy(
            src_ref=src, dst_ref=dst,
            send_sem=ring_send.at[r, i, way], recv_sem=ring_recv.at[r, i, way],
            device_id={"front": ahead if way == 0 else behind}, device_id_type=MESH,
        )

    def ring_in(r, i, way, who):
        hop, half = PIECES[i]
        half = half if way == 0 else 1 - half
        chip = (z + NZ - hop) % NZ if way == 0 else (z + hop) % NZ
        return blocks[r].at[place(chip, who, half)]

    def wait_ring(r, i, way):
        here = ring_in(r, i, way, core)
        pltpu.make_async_remote_copy(
            src_ref=here, dst_ref=here,
            send_sem=ring_send.at[r, i, way], recv_sem=ring_recv.at[r, i, way],
            device_id={"front": ahead}, device_id_type=MESH,
        ).wait_recv()

    def pair(r, i, way, who):
        here = ring_in(r, i, way, who)
        return pltpu.make_async_remote_copy(
            src_ref=here, dst_ref=here,
            send_sem=pair_send.at[r, i, way], recv_sem=pair_recv.at[r, i, way],
            device_id={"front": sibling}, device_id_type=MESH,
        )

    def pair_own(r, who):
        return pltpu.make_async_remote_copy(
            src_ref=parent.at[:, :, chunk_cols(r)],
            dst_ref=blocks[r].at[pl.ds((z * 2 + who) * OWNED, OWNED)],
            send_sem=pair_send.at[r, NP, 0], recv_sem=pair_recv.at[r, NP, 0],
            device_id={"front": sibling}, device_id_type=MESH,
        )

    def keep_own(r):
        return pltpu.make_async_copy(
            parent.at[:, :, chunk_cols(r)], blocks[r].at[pl.ds(front * OWNED, OWNED)], own_sem.at[r]
        )

    def scatter(r, k):
        return pltpu.make_async_remote_copy(
            src_ref=part.at[r, peer(k)], dst_ref=arrived.at[r, k],
            send_sem=tile_send.at[r, k], recv_sem=tile_recv.at[r, k],
            device_id={"tile": peer(k)}, device_id_type=MESH,
        )

    loads = [
        pltpu.make_async_copy(bases, bases_v, load_sem.at[0]),
        pltpu.make_async_copy(cols, cols_v, load_sem.at[1]),
        pltpu.make_async_copy(diag, diag_v, load_sem.at[2]),
        pltpu.make_async_copy(right_side, right_v, load_sem.at[3]),
    ]

    for i in (0, 1):
        for way in (0, 1):
            ring(0, i, way).start()
    pair_own(0, core).start()
    keep_own(0).start()
    for load in loads:
        load.start()
    for r in range(CHUNKS):
        blocks[r][NBLK] = jnp.zeros((BLOCK, WIDTH), jnp.bfloat16)

    def slot(c, q):
        s = c * SEG + q
        return jnp.where(q < counts[front, c], ids[front, s], NBLK)

    def sums(r, dy):
        to_y = (y + dy) % NY
        rows = pl.ds(pl.multiple_of(to_y * GROUP, GROUP), GROUP)
        for c in range(FRONTS):
            total = jnp.zeros((GROUP, WIDTH), jnp.float32)
            for q in range(SEG):
                total += jnp.dot(
                    bases_v[c, q, rows, :], blocks[r][slot(c, q)], preferred_element_type=jnp.float32
                )
            part[r, pl.ds(to_y * NX, NX), c] = total.astype(jnp.bfloat16).reshape(NX, RANK, WIDTH)
        for dx in range(NX):
            k = dy * NX + dx
            if k:
                scatter(r, k).start()

    def chunk_ready(r):
        for i in range(NP):
            for way in (0, 1):
                pair(r, i, way, 1 - core).wait_recv()
        pair_own(r, 1 - core).wait_recv()
        keep_own(r).wait()
        if r == 0:
            loads[0].wait()

    def out_copy(r):
        return pltpu.make_async_copy(out_v.at[r], out.at[:, :, chunk_cols(r)], out_sem.at[r])

    def finish(r):
        if r == 0:
            for load in loads[1:]:
                load.wait()
        for k in range(1, NT):
            scatter(r, k).wait_recv()
        arrived[r, 0] = part[r, tile]
        for c in range(FRONTS):
            total = jnp.sum(arrived[r, :, c].astype(jnp.float32), axis=0)
            row = lax.broadcasted_iota(jnp.int32, (RANK, WIDTH), 0)
            rank_space = jnp.where(row < ranks[c], total, 0.0).astype(jnp.bfloat16)
            projected = lax.dot_general(
                cols_v[c], rank_space, (((0,), (0,)), ((), ())), preferred_element_type=jnp.float32
            )
            reduced = (right_v[c, :, chunk_cols(r)].astype(jnp.float32) - projected).astype(jnp.bfloat16)
            out_v[r, c] = jnp.dot(
                diag_v[c], reduced, preferred_element_type=jnp.float32
            ).astype(jnp.bfloat16)
        out_copy(r).start()

    def sent(r):
        for i in range(NP):
            for way in (0, 1):
                ring(r, i, way).wait_send()
                pair(r, i, way, core).wait_send()
        pair_own(r, core).wait_send()

    order = (2, 1, 3, 0)
    for r in range(CHUNKS):
        for i in range(NP):
            for way in (0, 1):
                wait_ring(r, i, way)
                if i + 2 < NP:
                    ring(r, i + 2, way).start()
                elif r + 1 < CHUNKS:
                    ring(r + 1, i + 2 - NP, way).start()
                pair(r, i, way, core).start()
            if i == 0 and r + 1 < CHUNKS:
                pair_own(r + 1, core).start()
                keep_own(r + 1).start()
            if r >= 1:
                if i == 0:
                    chunk_ready(r - 1)
                if i < NY:
                    sums(r - 1, order[i])
            if r >= 2 and i == 4:
                finish(r - 2)
            if r >= 1 and i == 5:
                sent(r - 1)
    last = CHUNKS - 1
    chunk_ready(last)
    for dy in order:
        sums(last, dy)
    finish(last - 1)
    sent(last)
    for r in range(CHUNKS - 1):
        for k in range(1, NT):
            scatter(r, k).wait_send()
    finish(last)
    for k in range(1, NT):
        scatter(last, k).wait_send()
    for r in range(CHUNKS):
        out_copy(r).wait()


def local(
    parent_solution, segment_ids, segment_counts, row_bases, column_bases, diag_inverse, child_right, tile_ranks
):
    bases = row_bases.reshape(FRONTS, SEG, NT * RANK, BLOCK)
    whole = pl.BlockSpec(memory_space=pl.ANY)
    scalars = pl.BlockSpec(memory_space=pltpu.SMEM)
    dma = pltpu.SemaphoreType.DMA
    result = pl.pallas_call(
        kernel,
        out_shape=jax.ShapeDtypeStruct((FRONTS, BLOCK, RHS), jnp.bfloat16),
        in_specs=[scalars] * 3 + [whole] * 5,
        out_specs=whole,
        scratch_shapes=[pltpu.VMEM((NBLK + 1, BLOCK, WIDTH), jnp.bfloat16)] * CHUNKS
        + [
            pltpu.VMEM((FRONTS, SEG, NT * RANK, BLOCK), jnp.bfloat16),
            pltpu.VMEM((FRONTS, RANK, BLOCK), jnp.bfloat16),
            pltpu.VMEM((FRONTS, BLOCK, BLOCK), jnp.bfloat16),
            pltpu.VMEM((FRONTS, BLOCK, RHS), jnp.bfloat16),
            pltpu.VMEM((CHUNKS, FRONTS, BLOCK, WIDTH), jnp.bfloat16),
            pltpu.VMEM((CHUNKS, NT, FRONTS, RANK, WIDTH), jnp.bfloat16),
            pltpu.VMEM((CHUNKS, NT, FRONTS, RANK, WIDTH), jnp.bfloat16),
            dma((CHUNKS, NP, 2)),
            dma((CHUNKS, NP, 2)),
            dma((CHUNKS, NP + 1, 2)),
            dma((CHUNKS, NP + 1, 2)),
            dma((CHUNKS, NT)),
            dma((CHUNKS, NT)),
            dma((4,)),
            dma((CHUNKS,)),
            dma((CHUNKS,)),
        ],
        compiler_params=pltpu.CompilerParams(
            collective_id=0, has_side_effects=True, vmem_limit_bytes=56 * 1024 * 1024
        ),
        cost_estimate=pl.CostEstimate(
            flops=2 * FRONTS * SEG * NT * RANK * BLOCK * RHS, bytes_accessed=12 << 20, transcendentals=0
        ),
    )(
        segment_ids[0], segment_counts[0], tile_ranks.reshape(FRONTS),
        parent_solution[0], bases, column_bases[0, :, 0], diag_inverse[0, :, 0], child_right[0, :, 0],
    )
    return result[None, :, None]


def solution(mesh):
    placed = (
        P("tile", "front", None, None),
        P("tile", None, None),
        P("tile", None, None),
        P("tile", "front", None, None, None, None, None),
        P("front", None, "tile", None, None),
        P("front", None, "tile", None, None),
        P("front", None, "tile", None, None),
        P("front", None, "tile"),
    )
    return jax.shard_map(
        local,
        mesh=mesh,
        in_specs=placed,
        out_specs=P("front", None, "tile", None, None),
        check_vma=False,
    )
```

```python
import functools

import jax
import jax.numpy as jnp
from jax import lax
from jax.experimental import pallas as pl
from jax.experimental.pallas import tpu as pltpu
from jax.sharding import PartitionSpec as P

MESH = pl.DeviceIdType.MESH

NZ = 8
NY = 4
NX = 4
NT = NY * NX
OWNED = 4
BLOCK = 256
RANK = 64
RHS = 512
SEG = 8
FRONTS = 2
WIDTH = 128
CHUNKS = RHS // WIDTH
NBLK = NZ * 2 * OWNED
GROUP = NX * RANK
PIECES = ((1, 0), (1, 1), (2, 0), (2, 1), (3, 0), (3, 1), (4, 0))
NP = len(PIECES)


def kernel(
    ids, counts, ranks, parent, bases, cols, diag, right_side, out,
    b0, b1, b2, b3, bases_v, cols_v, diag_v, right_v, out_v, part, arrived,
    ring_send, ring_recv, pair_send, pair_recv, tile_send, tile_recv, load_sem, own_sem, out_sem,
):
    blocks = (b0, b1, b2, b3)
    front = lax.axis_index("front")
    tile = lax.axis_index("tile")
    z, core = front // 2, front % 2
    y, x = tile // NX, tile % NX
    sibling = z * 2 + (1 - core)
    ahead = ((z + 1) % NZ) * 2 + core
    behind = ((z + NZ - 1) % NZ) * 2 + core

    def peer(k):
        return ((y + k // NX) % NY) * NX + (x + k % NX) % NX

    barrier = pltpu.get_barrier_semaphore()
    for other in (ahead, behind, sibling):
        pl.semaphore_signal(barrier, inc=1, device_id={"front": other}, device_id_type=MESH)
    for k in range(1, NT):
        pl.semaphore_signal(barrier, inc=1, device_id={"tile": peer(k)}, device_id_type=MESH)
    pl.semaphore_wait(barrier, 3 + NT - 1)

    def place(chip, half):
        return pl.ds((chip * 2 + core) * OWNED + half * 2, 2)

    def chunk_cols(r):
        return pl.ds(r * WIDTH, WIDTH)

    def ring(r, i, way):
        hop, half = PIECES[i]
        half = half if way == 0 else 1 - half
        chip = (z + NZ - (hop - 1)) % NZ if way == 0 else (z + hop - 1) % NZ
        dst = blocks[r].at[place(chip, half)]
        if hop == 1:
            src = parent.at[pl.ds(half * 2, 2), :, chunk_cols(r)]
        else:
            src = dst
        return pltpu.make_async_remote_copy(
            src_ref=src, dst_ref=dst,
            send_sem=ring_send.at[r], recv_sem=ring_recv.at[r, i, way],
            device_id={"front": ahead if way == 0 else behind}, device_id_type=MESH,
        )

    def ring_in(r, i, way):
        hop, half = PIECES[i]
        half = half if way == 0 else 1 - half
        chip = (z + NZ - hop) % NZ if way == 0 else (z + hop) % NZ
        return blocks[r].at[place(chip, half)]

    def wait_ring(r, i, way):
        here = ring_in(r, i, way)
        pltpu.make_async_remote_copy(
            src_ref=here, dst_ref=here,
            send_sem=ring_send.at[r], recv_sem=ring_recv.at[r, i, way],
            device_id={"front": ahead}, device_id_type=MESH,
        ).wait_recv()

    def pair(r, i, way):
        here = ring_in(r, i, way)
        return pltpu.make_async_remote_copy(
            src_ref=here, dst_ref=here,
            send_sem=pair_send.at[r], recv_sem=pair_recv.at[r],
            device_id={"front": sibling}, device_id_type=MESH,
        )

    def pair_own(r):
        return pltpu.make_async_remote_copy(
            src_ref=parent.at[:, :, chunk_cols(r)],
            dst_ref=blocks[r].at[pl.ds(front * OWNED, OWNED)],
            send_sem=pair_send.at[r], recv_sem=pair_recv.at[r],
            device_id={"front": sibling}, device_id_type=MESH,
        )

    def keep_own(r):
        return pltpu.make_async_copy(
            parent.at[:, :, chunk_cols(r)], blocks[r].at[pl.ds(front * OWNED, OWNED)], own_sem.at[r]
        )

    def all_of(ref, send, recv):
        return pltpu.make_async_remote_copy(
            src_ref=ref, dst_ref=ref, send_sem=send, recv_sem=recv,
            device_id={"front": sibling}, device_id_type=MESH,
        )

    def all_ring(r):
        return all_of(blocks[r].at[pl.ds(0, 4 * NP)], ring_send.at[r], ring_recv.at[r, 0, 0])

    def all_pair(r):
        return all_of(blocks[r].at[pl.ds(0, 4 * NP + OWNED)], pair_send.at[r], pair_recv.at[r])

    def all_scatter(r):
        return all_of(arrived.at[r, pl.ds(1, NT - 1)], tile_send.at[r], tile_recv.at[r])

    def scatter(r, k):
        return pltpu.make_async_remote_copy(
            src_ref=part.at[r, peer(k)], dst_ref=arrived.at[r, k],
            send_sem=tile_send.at[r], recv_sem=tile_recv.at[r],
            device_id={"tile": peer(k)}, device_id_type=MESH,
        )

    loads = [
        pltpu.make_async_copy(bases, bases_v, load_sem.at[0]),
        pltpu.make_async_copy(cols, cols_v, load_sem.at[1]),
        pltpu.make_async_copy(diag, diag_v, load_sem.at[2]),
        pltpu.make_async_copy(right_side, right_v, load_sem.at[3]),
    ]

    for i in (0, 1):
        for way in (0, 1):
            ring(0, i, way).start()
    pair_own(0).start()
    keep_own(0).start()
    for load in loads:
        load.start()
    for r in range(CHUNKS):
        blocks[r][NBLK] = jnp.zeros((BLOCK, WIDTH), jnp.bfloat16)

    def slot(c, q):
        s = c * SEG + q
        return jnp.where(q < counts[c, front], ids[front, s], NBLK)

    def sums(r, dy):
        to_y = (y + dy) % NY
        rows = pl.ds(pl.multiple_of(to_y * GROUP, GROUP), GROUP)
        for c in range(FRONTS):
            total = jnp.zeros((GROUP, WIDTH), jnp.float32)
            for q in range(SEG):
                total += jnp.dot(
                    bases_v[c, q, rows, :], blocks[r][slot(c, q)], preferred_element_type=jnp.float32
                )
            part[r, pl.ds(to_y * NX, NX), c] = total.astype(jnp.bfloat16).reshape(NX, RANK, WIDTH)
        for dx in range(NX):
            k = dy * NX + dx
            if k:
                scatter(r, k).start()

    def chunk_ready(r):
        all_pair(r).wait_recv()
        keep_own(r).wait()
        if r == 0:
            loads[0].wait()

    def out_copy(r):
        return pltpu.make_async_copy(out_v.at[r], out.at[:, :, chunk_cols(r)], out_sem.at[r])

    def finish(r):
        if r == 0:
            for load in loads[1:]:
                load.wait()
        all_scatter(r).wait_recv()
        arrived[r, 0] = part[r, tile]
        for c in range(FRONTS):
            total = jnp.sum(arrived[r, :, c].astype(jnp.float32), axis=0)
            row = lax.broadcasted_iota(jnp.int32, (RANK, WIDTH), 0)
            rank_space = jnp.where(row < ranks[c], total, 0.0).astype(jnp.bfloat16)
            projected = lax.dot_general(
                cols_v[c], rank_space, (((0,), (0,)), ((), ())), preferred_element_type=jnp.float32
            )
            reduced = (right_v[c, :, chunk_cols(r)].astype(jnp.float32) - projected).astype(jnp.bfloat16)
            out_v[r, c] = jnp.dot(
                diag_v[c], reduced, preferred_element_type=jnp.float32
            ).astype(jnp.bfloat16)
        out_copy(r).start()

    def sent(r):
        all_ring(r).wait_send()
        all_pair(r).wait_send()

    order = (2, 1, 3, 0)
    for r in range(CHUNKS):
        for i in range(NP):
            for way in (0, 1):
                wait_ring(r, i, way)
                if i + 2 < NP:
                    ring(r, i + 2, way).start()
                elif r + 1 < CHUNKS:
                    ring(r + 1, i + 2 - NP, way).start()
                pair(r, i, way).start()
            if i == 0 and r + 1 < CHUNKS:
                pair_own(r + 1).start()
                keep_own(r + 1).start()
            if r >= 1:
                if i == 0:
                    chunk_ready(r - 1)
                if i < NY:
                    sums(r - 1, order[i])
            if r >= 2 and i == 4:
                finish(r - 2)
            if r >= 1 and i == 5:
                sent(r - 1)
    last = CHUNKS - 1
    chunk_ready(last)
    for dy in order:
        sums(last, dy)
    finish(last - 1)
    sent(last)
    for r in range(CHUNKS - 1):
        all_scatter(r).wait_send()
    finish(last)
    all_scatter(last).wait_send()
    for r in range(CHUNKS):
        out_copy(r).wait()


def local(
    parent_solution, segment_ids, segment_counts, row_bases, column_bases, diag_inverse, child_right, tile_ranks
):
    bases = row_bases.reshape(FRONTS, SEG, NT * RANK, BLOCK)
    whole = pl.BlockSpec(memory_space=pl.ANY)
    scalars = pl.BlockSpec(memory_space=pltpu.SMEM)
    dma = pltpu.SemaphoreType.DMA
    result = pl.pallas_call(
        kernel,
        out_shape=jax.ShapeDtypeStruct((FRONTS, BLOCK, RHS), jnp.bfloat16),
        in_specs=[scalars] * 3 + [whole] * 5,
        out_specs=whole,
        scratch_shapes=[pltpu.VMEM((NBLK + 1, BLOCK, WIDTH), jnp.bfloat16)] * CHUNKS
        + [
            pltpu.VMEM((FRONTS, SEG, NT * RANK, BLOCK), jnp.bfloat16),
            pltpu.VMEM((FRONTS, RANK, BLOCK), jnp.bfloat16),
            pltpu.VMEM((FRONTS, BLOCK, BLOCK), jnp.bfloat16),
            pltpu.VMEM((FRONTS, BLOCK, RHS), jnp.bfloat16),
            pltpu.VMEM((CHUNKS, FRONTS, BLOCK, WIDTH), jnp.bfloat16),
            pltpu.VMEM((CHUNKS, NT, FRONTS, RANK, WIDTH), jnp.bfloat16),
            pltpu.VMEM((CHUNKS, NT, FRONTS, RANK, WIDTH), jnp.bfloat16),
            dma((CHUNKS,)),
            dma((CHUNKS, NP, 2)),
            dma((CHUNKS,)),
            dma((CHUNKS,)),
            dma((CHUNKS,)),
            dma((CHUNKS,)),
            dma((4,)),
            dma((CHUNKS,)),
            dma((CHUNKS,)),
        ],
        compiler_params=pltpu.CompilerParams(
            collective_id=0, has_side_effects=True, vmem_limit_bytes=56 * 1024 * 1024
        ),
        cost_estimate=pl.CostEstimate(
            flops=2 * FRONTS * SEG * NT * RANK * BLOCK * RHS, bytes_accessed=12 << 20, transcendentals=0
        ),
    )(
        segment_ids[0], segment_counts[0].T, tile_ranks.reshape(FRONTS),
        parent_solution[0], bases, column_bases[0, :, 0], diag_inverse[0, :, 0], child_right[0, :, 0],
    )
    return result[None, :, None]


def solution(mesh):
    placed = (
        P("tile", "front", None, None),
        P("tile", None, None),
        P("tile", None, None),
        P("tile", "front", None, None, None, None, None),
        P("front", None, "tile", None, None),
        P("front", None, "tile", None, None),
        P("front", None, "tile", None, None),
        P("front", None, "tile"),
    )
    return jax.shard_map(
        local,
        mesh=mesh,
        in_specs=placed,
        out_specs=P("front", None, "tile", None, None),
        check_vma=False,
    )
```

```python
import functools

import jax
import jax.numpy as jnp
from jax import lax
from jax.experimental import pallas as pl
from jax.experimental.pallas import tpu as pltpu
from jax.sharding import PartitionSpec as P

MESH = pl.DeviceIdType.MESH

NZ = 8
NY = 4
NX = 4
NT = NY * NX
OWNED = 4
BLOCK = 256
RANK = 64
RHS = 512
SEG = 8
FRONTS = 2
WIDTH = 128
CHUNKS = RHS // WIDTH
NBLK = NZ * 2 * OWNED
GROUP = NX * RANK
PIECES = ((1, 0), (1, 1), (2, 0), (2, 1), (3, 0), (3, 1), (4, 0))
NP = len(PIECES)


def kernel(
    ids, counts, ranks, parent, bases, cols, diag, right_side, out,
    b0, b1, b2, b3, bases_v, cols_v, diag_v, right_v, part, arrived,
    ring_send, ring_recv, pair_send, pair_recv, tile_send, tile_recv, load_sem, own_sem, row_sem,
):
    blocks = (b0, b1, b2, b3)
    front = lax.axis_index("front")
    tile = lax.axis_index("tile")
    z, core = front // 2, front % 2
    y, x = tile // NX, tile % NX
    sibling = z * 2 + (1 - core)
    ahead = ((z + 1) % NZ) * 2 + core
    behind = ((z + NZ - 1) % NZ) * 2 + core

    def peer(k):
        return ((y + k // NX) % NY) * NX + (x + k % NX) % NX

    barrier = pltpu.get_barrier_semaphore()
    for other in (ahead, behind, sibling):
        pl.semaphore_signal(barrier, inc=1, device_id={"front": other}, device_id_type=MESH)
    along_x = (peer(1), peer(NX - 1))
    along_y = (peer(NX), peer((NY - 1) * NX))
    for other in along_x + along_y:
        pl.semaphore_signal(barrier, inc=1, device_id={"tile": other}, device_id_type=MESH)
    pl.semaphore_wait(barrier, 3 + 4)

    def tell(step):
        for other in along_x if step == 0 else along_y:
            pl.semaphore_signal(row_sem.at[step], inc=1, device_id={"tile": other}, device_id_type=MESH)

    def told(step):
        pl.semaphore_wait(row_sem.at[step], 2)

    def place(chip, half):
        return pl.ds((chip * 2 + core) * OWNED + half * 2, 2)

    def chunk_cols(r):
        return pl.ds(r * WIDTH, WIDTH)

    def ring(r, i, way):
        hop, half = PIECES[i]
        half = half if way == 0 else 1 - half
        chip = (z + NZ - (hop - 1)) % NZ if way == 0 else (z + hop - 1) % NZ
        dst = blocks[r].at[place(chip, half)]
        if hop == 1:
            src = parent.at[pl.ds(half * 2, 2), :, chunk_cols(r)]
        else:
            src = dst
        return pltpu.make_async_remote_copy(
            src_ref=src, dst_ref=dst,
            send_sem=ring_send.at[r], recv_sem=ring_recv.at[r, i, way],
            device_id={"front": ahead if way == 0 else behind}, device_id_type=MESH,
        )

    def ring_in(r, i, way):
        hop, half = PIECES[i]
        half = half if way == 0 else 1 - half
        chip = (z + NZ - hop) % NZ if way == 0 else (z + hop) % NZ
        return blocks[r].at[place(chip, half)]

    def wait_ring(r, i, way):
        here = ring_in(r, i, way)
        pltpu.make_async_remote_copy(
            src_ref=here, dst_ref=here,
            send_sem=ring_send.at[r], recv_sem=ring_recv.at[r, i, way],
            device_id={"front": ahead}, device_id_type=MESH,
        ).wait_recv()

    def pair(r, i, way):
        here = ring_in(r, i, way)
        return pltpu.make_async_remote_copy(
            src_ref=here, dst_ref=here,
            send_sem=pair_send.at[r], recv_sem=pair_recv.at[r],
            device_id={"front": sibling}, device_id_type=MESH,
        )

    def pair_own(r):
        return pltpu.make_async_remote_copy(
            src_ref=parent.at[:, :, chunk_cols(r)],
            dst_ref=blocks[r].at[pl.ds(front * OWNED, OWNED)],
            send_sem=pair_send.at[r], recv_sem=pair_recv.at[r],
            device_id={"front": sibling}, device_id_type=MESH,
        )

    def keep_own(r):
        return pltpu.make_async_copy(
            parent.at[:, :, chunk_cols(r)], blocks[r].at[pl.ds(front * OWNED, OWNED)], own_sem.at[r]
        )

    def all_of(ref, send, recv):
        return pltpu.make_async_remote_copy(
            src_ref=ref, dst_ref=ref, send_sem=send, recv_sem=recv,
            device_id={"front": sibling}, device_id_type=MESH,
        )

    def all_ring(r):
        return all_of(blocks[r].at[pl.ds(0, 4 * NP)], ring_send.at[r], ring_recv.at[r, 0, 0])

    def all_pair(r):
        return all_of(blocks[r].at[pl.ds(0, 4 * NP + OWNED)], pair_send.at[r], pair_recv.at[r])

    def all_scatter(r):
        return all_of(arrived.at[r, pl.ds(1, NT - 1)], tile_send.at[r], tile_recv.at[r])

    def scatter(r, k):
        return pltpu.make_async_remote_copy(
            src_ref=part.at[r, peer(k)], dst_ref=arrived.at[r, k],
            send_sem=tile_send.at[r], recv_sem=tile_recv.at[r],
            device_id={"tile": peer(k)}, device_id_type=MESH,
        )

    loads = [
        pltpu.make_async_copy(bases, bases_v, load_sem.at[0]),
        pltpu.make_async_copy(cols, cols_v, load_sem.at[1]),
        pltpu.make_async_copy(diag, diag_v, load_sem.at[2]),
        pltpu.make_async_copy(right_side, right_v, load_sem.at[3]),
    ]

    for i in (0, 1):
        for way in (0, 1):
            ring(0, i, way).start()
    pair_own(0).start()
    keep_own(0).start()
    for load in loads:
        load.start()
    tell(0)
    for r in range(CHUNKS):
        blocks[r][NBLK] = jnp.zeros((BLOCK, WIDTH), jnp.bfloat16)

    def slot(c, q):
        s = c * SEG + q
        return jnp.where(q < counts[c, front], ids[front, s], NBLK)

    def sums(r, dy):
        to_y = (y + dy) % NY
        rows = pl.ds(pl.multiple_of(to_y * GROUP, GROUP), GROUP)
        for c in range(FRONTS):
            total = jnp.zeros((GROUP, WIDTH), jnp.float32)
            for q in range(SEG):
                total += jnp.dot(
                    bases_v[c, q, rows, :], blocks[r][slot(c, q)], preferred_element_type=jnp.float32
                )
            part[r, pl.ds(to_y * NX, NX), c] = total.astype(jnp.bfloat16).reshape(NX, RANK, WIDTH)
        for dx in range(NX):
            k = dy * NX + dx
            if k:
                scatter(r, k).start()

    def chunk_ready(r):
        all_pair(r).wait_recv()
        keep_own(r).wait()
        if r == 0:
            loads[0].wait()

    def finish(r):
        if r == 0:
            for load in loads[1:]:
                load.wait()
        all_scatter(r).wait_recv()
        arrived[r, 0] = part[r, tile]
        for c in range(FRONTS):
            total = jnp.sum(arrived[r, :, c].astype(jnp.float32), axis=0)
            row = lax.broadcasted_iota(jnp.int32, (RANK, WIDTH), 0)
            rank_space = jnp.where(row < ranks[c], total, 0.0).astype(jnp.bfloat16)
            projected = lax.dot_general(
                cols_v[c], rank_space, (((0,), (0,)), ((), ())), preferred_element_type=jnp.float32
            )
            reduced = (right_v[c, :, chunk_cols(r)].astype(jnp.float32) - projected).astype(jnp.bfloat16)
            out[c, :, chunk_cols(r)] = jnp.dot(
                diag_v[c], reduced, preferred_element_type=jnp.float32
            ).astype(jnp.bfloat16)

    def sent(r):
        all_ring(r).wait_send()
        all_pair(r).wait_send()

    order = (2, 1, 3, 0)
    for r in range(CHUNKS):
        for i in range(NP):
            for way in (0, 1):
                wait_ring(r, i, way)
                if i + 2 < NP:
                    ring(r, i + 2, way).start()
                elif r + 1 < CHUNKS:
                    ring(r + 1, i + 2 - NP, way).start()
                pair(r, i, way).start()
            if r == 0 and i < 3:
                told(i)
                if i < 2:
                    tell(i + 1)
            if i == 0 and r + 1 < CHUNKS:
                pair_own(r + 1).start()
                keep_own(r + 1).start()
            if r >= 1:
                if i == 0:
                    chunk_ready(r - 1)
                if i < NY:
                    sums(r - 1, order[i])
            if r >= 2 and i == 4:
                finish(r - 2)
            if r >= 1 and i == 5:
                sent(r - 1)
    last = CHUNKS - 1
    chunk_ready(last)
    for dy in order:
        sums(last, dy)
    finish(last - 1)
    sent(last)
    for r in range(CHUNKS - 1):
        all_scatter(r).wait_send()
    finish(last)
    all_scatter(last).wait_send()


def local(
    parent_solution, segment_ids, segment_counts, row_bases, column_bases, diag_inverse, child_right, tile_ranks
):
    bases = row_bases.reshape(FRONTS, SEG, NT * RANK, BLOCK)
    whole = pl.BlockSpec(memory_space=pl.ANY)
    scalars = pl.BlockSpec(memory_space=pltpu.SMEM)
    dma = pltpu.SemaphoreType.DMA
    result = pl.pallas_call(
        kernel,
        out_shape=pltpu.VMEM((FRONTS, BLOCK, RHS), jnp.bfloat16),
        in_specs=[scalars] * 3 + [whole] * 5,
        out_specs=pl.BlockSpec(memory_space=pltpu.VMEM),
        scratch_shapes=[pltpu.VMEM((NBLK + 1, BLOCK, WIDTH), jnp.bfloat16)] * CHUNKS
        + [
            pltpu.VMEM((FRONTS, SEG, NT * RANK, BLOCK), jnp.bfloat16),
            pltpu.VMEM((FRONTS, RANK, BLOCK), jnp.bfloat16),
            pltpu.VMEM((FRONTS, BLOCK, BLOCK), jnp.bfloat16),
            pltpu.VMEM((FRONTS, BLOCK, RHS), jnp.bfloat16),
            pltpu.VMEM((CHUNKS, NT, FRONTS, RANK, WIDTH), jnp.bfloat16),
            pltpu.VMEM((CHUNKS, NT, FRONTS, RANK, WIDTH), jnp.bfloat16),
            dma((CHUNKS,)),
            dma((CHUNKS, NP, 2)),
            dma((CHUNKS,)),
            dma((CHUNKS,)),
            dma((CHUNKS,)),
            dma((CHUNKS,)),
            dma((4,)),
            dma((CHUNKS,)),
            pltpu.SemaphoreType.REGULAR((3,)),
        ],
        compiler_params=pltpu.CompilerParams(
            collective_id=0, has_side_effects=True, vmem_limit_bytes=56 * 1024 * 1024
        ),
        cost_estimate=pl.CostEstimate(
            flops=2 * FRONTS * SEG * NT * RANK * BLOCK * RHS, bytes_accessed=12 << 20, transcendentals=0
        ),
    )(
        segment_ids[0], segment_counts[0].T, tile_ranks.reshape(FRONTS),
        parent_solution[0], bases, column_bases[0, :, 0], diag_inverse[0, :, 0], child_right[0, :, 0],
    )
    return result[None, :, None]


def solution(mesh):
    placed = (
        P("tile", "front", None, None),
        P("tile", None, None),
        P("tile", None, None),
        P("tile", "front", None, None, None, None, None),
        P("front", None, "tile", None, None),
        P("front", None, "tile", None, None),
        P("front", None, "tile", None, None),
        P("front", None, "tile"),
    )
    return jax.shard_map(
        local,
        mesh=mesh,
        in_specs=placed,
        out_specs=P("front", None, "tile", None, None),
        check_vma=False,
    )
```

```python
import functools

import jax
import jax.numpy as jnp
from jax import lax
from jax.experimental import pallas as pl
from jax.experimental.pallas import tpu as pltpu
from jax.sharding import PartitionSpec as P

MESH = pl.DeviceIdType.MESH

NZ = 8
NY = 4
NX = 4
NT = NY * NX
OWNED = 4
BLOCK = 256
RANK = 64
RHS = 512
SEG = 8
FRONTS = 2
WIDTH = 128
CHUNKS = RHS // WIDTH
NBLK = NZ * 2 * OWNED
GROUP = NX * RANK
PIECES = ((1, 0), (1, 1), (2, 0), (2, 1), (3, 0), (3, 1), (4, 0))
NP = len(PIECES)


def kernel(
    ids, counts, ranks, parent, bases, cols, diag, right_side, out,
    b0, b1, b2, b3, bases_v, cols_v, diag_v, right_v, part, arrived,
    ring_send, ring_recv, pair_send, pair_recv, tile_send, tile_recv, load_sem, own_sem, row_sem,
):
    blocks = (b0, b1, b2, b3)
    front = lax.axis_index("front")
    tile = lax.axis_index("tile")
    z, core = front // 2, front % 2
    y, x = tile // NX, tile % NX
    sibling = z * 2 + (1 - core)
    ahead = ((z + 1) % NZ) * 2 + core
    behind = ((z + NZ - 1) % NZ) * 2 + core

    def peer(k):
        return ((y + k // NX) % NY) * NX + (x + k % NX) % NX

    barrier = pltpu.get_barrier_semaphore()
    for other in (ahead, behind, sibling):
        pl.semaphore_signal(barrier, inc=1, device_id={"front": other}, device_id_type=MESH)
    along_x = (peer(1), peer(NX - 1))
    along_y = (peer(NX), peer((NY - 1) * NX))
    ground = z == 0

    @pl.when(ground)
    def _():
        for other in along_x + along_y:
            pl.semaphore_signal(barrier, inc=1, device_id={"tile": other}, device_id_type=MESH)

    pl.semaphore_wait(barrier, jnp.where(ground, 3 + 4, 3))

    def tell(step):
        for other in along_x if step == 0 else along_y:
            pl.semaphore_signal(row_sem.at[step], inc=1, device_id={"tile": other}, device_id_type=MESH)

    def told(step):
        pl.semaphore_wait(row_sem.at[step], 2)
        if step < 2:
            tell(step + 1)

    def column_entered():
        for k in range(1, NT):
            pl.semaphore_signal(row_sem.at[3], inc=1, device_id={"tile": peer(k)}, device_id_type=MESH)

    def all_entered():
        pl.semaphore_wait(row_sem.at[3], NT - 1)
        for chip in range(1, NZ):
            pl.semaphore_signal(
                row_sem.at[4], inc=1, device_id={"front": chip * 2 + core}, device_id_type=MESH
            )

    def place(chip, half):
        return pl.ds((chip * 2 + core) * OWNED + half * 2, 2)

    def chunk_cols(r):
        return pl.ds(r * WIDTH, WIDTH)

    def ring(r, i, way):
        hop, half = PIECES[i]
        half = half if way == 0 else 1 - half
        chip = (z + NZ - (hop - 1)) % NZ if way == 0 else (z + hop - 1) % NZ
        dst = blocks[r].at[place(chip, half)]
        if hop == 1:
            src = parent.at[pl.ds(half * 2, 2), :, chunk_cols(r)]
        else:
            src = dst
        return pltpu.make_async_remote_copy(
            src_ref=src, dst_ref=dst,
            send_sem=ring_send.at[r], recv_sem=ring_recv.at[r, i, way],
            device_id={"front": ahead if way == 0 else behind}, device_id_type=MESH,
        )

    def ring_in(r, i, way):
        hop, half = PIECES[i]
        half = half if way == 0 else 1 - half
        chip = (z + NZ - hop) % NZ if way == 0 else (z + hop) % NZ
        return blocks[r].at[place(chip, half)]

    def wait_ring(r, i, way):
        here = ring_in(r, i, way)
        pltpu.make_async_remote_copy(
            src_ref=here, dst_ref=here,
            send_sem=ring_send.at[r], recv_sem=ring_recv.at[r, i, way],
            device_id={"front": ahead}, device_id_type=MESH,
        ).wait_recv()

    def pair(r, i, way):
        here = ring_in(r, i, way)
        return pltpu.make_async_remote_copy(
            src_ref=here, dst_ref=here,
            send_sem=pair_send.at[r], recv_sem=pair_recv.at[r],
            device_id={"front": sibling}, device_id_type=MESH,
        )

    def pair_own(r):
        return pltpu.make_async_remote_copy(
            src_ref=parent.at[:, :, chunk_cols(r)],
            dst_ref=blocks[r].at[pl.ds(front * OWNED, OWNED)],
            send_sem=pair_send.at[r], recv_sem=pair_recv.at[r],
            device_id={"front": sibling}, device_id_type=MESH,
        )

    def keep_own(r):
        return pltpu.make_async_copy(
            parent.at[:, :, chunk_cols(r)], blocks[r].at[pl.ds(front * OWNED, OWNED)], own_sem.at[r]
        )

    def all_of(ref, send, recv):
        return pltpu.make_async_remote_copy(
            src_ref=ref, dst_ref=ref, send_sem=send, recv_sem=recv,
            device_id={"front": sibling}, device_id_type=MESH,
        )

    def all_ring(r):
        return all_of(blocks[r].at[pl.ds(0, 4 * NP)], ring_send.at[r], ring_recv.at[r, 0, 0])

    def all_pair(r):
        return all_of(blocks[r].at[pl.ds(0, 4 * NP + OWNED)], pair_send.at[r], pair_recv.at[r])

    def all_scatter(r):
        return all_of(arrived.at[r, pl.ds(1, NT - 1)], tile_send.at[r], tile_recv.at[r])

    def scatter(r, k):
        return pltpu.make_async_remote_copy(
            src_ref=part.at[r, peer(k)], dst_ref=arrived.at[r, k],
            send_sem=tile_send.at[r], recv_sem=tile_recv.at[r],
            device_id={"tile": peer(k)}, device_id_type=MESH,
        )

    loads = [
        pltpu.make_async_copy(bases, bases_v, load_sem.at[0]),
        pltpu.make_async_copy(cols, cols_v, load_sem.at[1]),
        pltpu.make_async_copy(diag, diag_v, load_sem.at[2]),
        pltpu.make_async_copy(right_side, right_v, load_sem.at[3]),
    ]

    for i in (0, 1):
        for way in (0, 1):
            ring(0, i, way).start()
    pair_own(0).start()
    keep_own(0).start()
    for load in loads:
        load.start()
    pl.when(ground)(lambda: tell(0))
    for r in range(CHUNKS):
        blocks[r][NBLK] = jnp.zeros((BLOCK, WIDTH), jnp.bfloat16)

    def slot(c, q):
        s = c * SEG + q
        return jnp.where(q < counts[c, front], ids[front, s], NBLK)

    def sums(r, dy):
        to_y = (y + dy) % NY
        rows = pl.ds(pl.multiple_of(to_y * GROUP, GROUP), GROUP)
        for c in range(FRONTS):
            total = jnp.zeros((GROUP, WIDTH), jnp.float32)
            for q in range(SEG):
                total += jnp.dot(
                    bases_v[c, q, rows, :], blocks[r][slot(c, q)], preferred_element_type=jnp.float32
                )
            part[r, pl.ds(to_y * NX, NX), c] = total.astype(jnp.bfloat16).reshape(NX, RANK, WIDTH)
        for dx in range(NX):
            k = dy * NX + dx
            if k:
                scatter(r, k).start()

    def chunk_ready(r):
        all_pair(r).wait_recv()
        keep_own(r).wait()
        if r == 0:
            loads[0].wait()

    def finish(r):
        if r == 0:
            for load in loads[1:]:
                load.wait()
        all_scatter(r).wait_recv()
        arrived[r, 0] = part[r, tile]
        for c in range(FRONTS):
            total = jnp.sum(arrived[r, :, c].astype(jnp.float32), axis=0)
            row = lax.broadcasted_iota(jnp.int32, (RANK, WIDTH), 0)
            rank_space = jnp.where(row < ranks[c], total, 0.0).astype(jnp.bfloat16)
            projected = lax.dot_general(
                cols_v[c], rank_space, (((0,), (0,)), ((), ())), preferred_element_type=jnp.float32
            )
            reduced = (right_v[c, :, chunk_cols(r)].astype(jnp.float32) - projected).astype(jnp.bfloat16)
            out[c, :, chunk_cols(r)] = jnp.dot(
                diag_v[c], reduced, preferred_element_type=jnp.float32
            ).astype(jnp.bfloat16)

    def sent(r):
        all_ring(r).wait_send()
        all_pair(r).wait_send()

    order = (2, 1, 3, 0)
    for r in range(CHUNKS):
        for i in range(NP):
            for way in (0, 1):
                wait_ring(r, i, way)
                if i + 2 < NP:
                    ring(r, i + 2, way).start()
                elif r + 1 < CHUNKS:
                    ring(r + 1, i + 2 - NP, way).start()
                pair(r, i, way).start()
            if r == 0 and i < 3:
                pl.when(ground)(functools.partial(told, i))
            if (r, i) == (0, 6):
                pl.when(ground)(column_entered)
            if (r, i) == (1, 1):
                pl.when(ground)(all_entered)
            if (r, i) == (1, 3):
                pl.when(z > 0)(lambda: pl.semaphore_wait(row_sem.at[4], 1))
            if i == 0 and r + 1 < CHUNKS:
                pair_own(r + 1).start()
                keep_own(r + 1).start()
            if r >= 1:
                if i == 0:
                    chunk_ready(r - 1)
                after = 3 if r == 1 else 0
                if after <= i < after + NY:
                    sums(r - 1, order[i - after])
            if r >= 2 and i == 4:
                finish(r - 2)
            if r >= 1 and i == 5:
                sent(r - 1)
    last = CHUNKS - 1
    chunk_ready(last)
    for dy in order:
        sums(last, dy)
    finish(last - 1)
    sent(last)
    for r in range(CHUNKS - 1):
        all_scatter(r).wait_send()
    finish(last)
    all_scatter(last).wait_send()


def local(
    parent_solution, segment_ids, segment_counts, row_bases, column_bases, diag_inverse, child_right, tile_ranks
):
    bases = row_bases.reshape(FRONTS, SEG, NT * RANK, BLOCK)
    whole = pl.BlockSpec(memory_space=pl.ANY)
    scalars = pl.BlockSpec(memory_space=pltpu.SMEM)
    dma = pltpu.SemaphoreType.DMA
    result = pl.pallas_call(
        kernel,
        out_shape=pltpu.VMEM((FRONTS, BLOCK, RHS), jnp.bfloat16),
        in_specs=[scalars] * 3 + [whole] * 5,
        out_specs=pl.BlockSpec(memory_space=pltpu.VMEM),
        scratch_shapes=[pltpu.VMEM((NBLK + 1, BLOCK, WIDTH), jnp.bfloat16)] * CHUNKS
        + [
            pltpu.VMEM((FRONTS, SEG, NT * RANK, BLOCK), jnp.bfloat16),
            pltpu.VMEM((FRONTS, RANK, BLOCK), jnp.bfloat16),
            pltpu.VMEM((FRONTS, BLOCK, BLOCK), jnp.bfloat16),
            pltpu.VMEM((FRONTS, BLOCK, RHS), jnp.bfloat16),
            pltpu.VMEM((CHUNKS, NT, FRONTS, RANK, WIDTH), jnp.bfloat16),
            pltpu.VMEM((CHUNKS, NT, FRONTS, RANK, WIDTH), jnp.bfloat16),
            dma((CHUNKS,)),
            dma((CHUNKS, NP, 2)),
            dma((CHUNKS,)),
            dma((CHUNKS,)),
            dma((CHUNKS,)),
            dma((CHUNKS,)),
            dma((4,)),
            dma((CHUNKS,)),
            pltpu.SemaphoreType.REGULAR((5,)),
        ],
        compiler_params=pltpu.CompilerParams(
            collective_id=0, has_side_effects=True, vmem_limit_bytes=56 * 1024 * 1024
        ),
        cost_estimate=pl.CostEstimate(
            flops=2 * FRONTS * SEG * NT * RANK * BLOCK * RHS, bytes_accessed=12 << 20, transcendentals=0
        ),
    )(
        segment_ids[0], segment_counts[0].T, tile_ranks.reshape(FRONTS),
        parent_solution[0], bases, column_bases[0, :, 0], diag_inverse[0, :, 0], child_right[0, :, 0],
    )
    return result[None, :, None]


def solution(mesh):
    placed = (
        P("tile", "front", None, None),
        P("tile", None, None),
        P("tile", None, None),
        P("tile", "front", None, None, None, None, None),
        P("front", None, "tile", None, None),
        P("front", None, "tile", None, None),
        P("front", None, "tile", None, None),
        P("front", None, "tile"),
    )
    return jax.shard_map(
        local,
        mesh=mesh,
        in_specs=placed,
        out_specs=P("front", None, "tile", None, None),
        check_vma=False,
    )
```

```python
import functools

import jax
import jax.numpy as jnp
from jax import lax
from jax.experimental import pallas as pl
from jax.experimental.pallas import tpu as pltpu
from jax.sharding import PartitionSpec as P

MESH = pl.DeviceIdType.MESH

NZ = 8
NY = 4
NX = 4
NT = NY * NX
OWNED = 4
BLOCK = 256
RANK = 64
RHS = 512
SEG = 8
FRONTS = 2
WIDTH = 128
CHUNKS = RHS // WIDTH
NBLK = NZ * 2 * OWNED
GROUP = NX * RANK
PIECES = ((1, 0, 2), (1, 2, 2), (2, 0, 2), (2, 2, 2), (3, 0, 2), (3, 2, 2), (4, 0, 2))
NP = len(PIECES)
LAST_PIECES = PIECES[:-1] + ((4, 0, 1), (4, 1, 1))


def kernel(
    ids, counts, ranks, parent, bases, cols, diag, right_side, out,
    b0, b1, b2, b3, bases_v, cols_v, diag_v, right_v, part, arrived,
    ring_send, ring_recv, pair_send, pair_recv, tile_send, tile_recv, load_sem, own_sem, row_sem,
):
    blocks = (b0, b1, b2, b3)
    front = lax.axis_index("front")
    tile = lax.axis_index("tile")
    z, core = front // 2, front % 2
    y, x = tile // NX, tile % NX
    sibling = z * 2 + (1 - core)
    ahead = ((z + 1) % NZ) * 2 + core
    behind = ((z + NZ - 1) % NZ) * 2 + core

    def peer(k):
        return ((y + k // NX) % NY) * NX + (x + k % NX) % NX

    barrier = pltpu.get_barrier_semaphore()
    for other in (ahead, behind, sibling):
        pl.semaphore_signal(barrier, inc=1, device_id={"front": other}, device_id_type=MESH)
    along_x = (peer(1), peer(NX - 1))
    along_y = (peer(NX), peer((NY - 1) * NX))
    ground = z == 0

    @pl.when(ground)
    def _():
        for other in along_x + along_y:
            pl.semaphore_signal(barrier, inc=1, device_id={"tile": other}, device_id_type=MESH)

    pl.semaphore_wait(barrier, jnp.where(ground, 3 + 4, 3))

    def tell(step):
        for other in along_x if step == 0 else along_y:
            pl.semaphore_signal(row_sem.at[step], inc=1, device_id={"tile": other}, device_id_type=MESH)

    def told(step):
        pl.semaphore_wait(row_sem.at[step], 2)
        if step < 2:
            tell(step + 1)

    def column_entered():
        for k in range(1, NT):
            pl.semaphore_signal(row_sem.at[3], inc=1, device_id={"tile": peer(k)}, device_id_type=MESH)

    def all_entered():
        pl.semaphore_wait(row_sem.at[3], NT - 1)
        for chip in range(1, NZ):
            pl.semaphore_signal(
                row_sem.at[4], inc=1, device_id={"front": chip * 2 + core}, device_id_type=MESH
            )

    def place(chip, first, size):
        return pl.ds((chip * 2 + core) * OWNED + first, size)

    def pieces(r):
        return PIECES if r < CHUNKS - 1 else LAST_PIECES

    def piece(r, i, way):
        hop, first, size = pieces(r)[i]
        return hop, first if way == 0 else OWNED - first - size, size

    def chunk_cols(r):
        return pl.ds(r * WIDTH, WIDTH)

    def ring(r, i, way):
        hop, first, size = piece(r, i, way)
        chip = (z + NZ - (hop - 1)) % NZ if way == 0 else (z + hop - 1) % NZ
        dst = blocks[r].at[place(chip, first, size)]
        if hop == 1:
            src = parent.at[pl.ds(first, size), :, chunk_cols(r)]
        else:
            src = dst
        return pltpu.make_async_remote_copy(
            src_ref=src, dst_ref=dst,
            send_sem=ring_send.at[r], recv_sem=ring_recv.at[r % 2, i, way],
            device_id={"front": ahead if way == 0 else behind}, device_id_type=MESH,
        )

    def ring_in(r, i, way):
        hop, first, size = piece(r, i, way)
        chip = (z + NZ - hop) % NZ if way == 0 else (z + hop) % NZ
        return blocks[r].at[place(chip, first, size)]

    def wait_ring(r, i, way):
        here = ring_in(r, i, way)
        pltpu.make_async_remote_copy(
            src_ref=here, dst_ref=here,
            send_sem=ring_send.at[r], recv_sem=ring_recv.at[r % 2, i, way],
            device_id={"front": ahead}, device_id_type=MESH,
        ).wait_recv()

    def pair(r, i, way):
        here = ring_in(r, i, way)
        return pltpu.make_async_remote_copy(
            src_ref=here, dst_ref=here,
            send_sem=pair_send.at[r], recv_sem=pair_recv.at[r],
            device_id={"front": sibling}, device_id_type=MESH,
        )

    def pair_own(r):
        return pltpu.make_async_remote_copy(
            src_ref=parent.at[:, :, chunk_cols(r)],
            dst_ref=blocks[r].at[pl.ds(front * OWNED, OWNED)],
            send_sem=pair_send.at[r], recv_sem=pair_recv.at[r],
            device_id={"front": sibling}, device_id_type=MESH,
        )

    def keep_own(r):
        return pltpu.make_async_copy(
            parent.at[:, :, chunk_cols(r)], blocks[r].at[pl.ds(front * OWNED, OWNED)], own_sem.at[r]
        )

    def all_of(ref, send, recv):
        return pltpu.make_async_remote_copy(
            src_ref=ref, dst_ref=ref, send_sem=send, recv_sem=recv,
            device_id={"front": sibling}, device_id_type=MESH,
        )

    def all_ring(r):
        return all_of(blocks[r].at[pl.ds(0, 4 * NP)], ring_send.at[r], ring_recv.at[r % 2, 0, 0])

    def all_pair(r):
        return all_of(blocks[r].at[pl.ds(0, 4 * NP + OWNED)], pair_send.at[r], pair_recv.at[r])

    def all_scatter(r):
        return all_of(arrived.at[r, pl.ds(1, NT - 1)], tile_send.at[r], tile_recv.at[r])

    def scatter(r, k):
        return pltpu.make_async_remote_copy(
            src_ref=part.at[r, peer(k)], dst_ref=arrived.at[r, k],
            send_sem=tile_send.at[r], recv_sem=tile_recv.at[r],
            device_id={"tile": peer(k)}, device_id_type=MESH,
        )

    loads = [
        pltpu.make_async_copy(bases, bases_v, load_sem.at[0]),
        pltpu.make_async_copy(cols, cols_v, load_sem.at[1]),
        pltpu.make_async_copy(diag, diag_v, load_sem.at[2]),
        pltpu.make_async_copy(right_side, right_v, load_sem.at[3]),
    ]

    for i in (0, 1):
        for way in (0, 1):
            ring(0, i, way).start()
    pair_own(0).start()
    keep_own(0).start()
    for load in loads:
        load.start()
    pl.when(ground)(lambda: tell(0))
    for r in range(CHUNKS):
        blocks[r][NBLK] = jnp.zeros((BLOCK, WIDTH), jnp.bfloat16)

    def slot(c, q):
        s = c * SEG + q
        return jnp.where(q < counts[c, front], ids[front, s], NBLK)

    def sums(r, dy):
        to_y = (y + dy) % NY
        rows = pl.ds(pl.multiple_of(to_y * GROUP, GROUP), GROUP)
        for c in range(FRONTS):
            total = jnp.zeros((GROUP, WIDTH), jnp.float32)
            for q in range(SEG):
                total += jnp.dot(
                    bases_v[c, q, rows, :], blocks[r][slot(c, q)], preferred_element_type=jnp.float32
                )
            part[r, pl.ds(to_y * NX, NX), c] = total.astype(jnp.bfloat16).reshape(NX, RANK, WIDTH)
        for dx in range(NX):
            k = dy * NX + dx
            if k:
                scatter(r, k).start()

    def chunk_ready(r):
        all_pair(r).wait_recv()
        keep_own(r).wait()
        if r == 0:
            loads[0].wait()

    def finish(r):
        if r == 0:
            for load in loads[1:]:
                load.wait()
        all_scatter(r).wait_recv()
        arrived[r, 0] = part[r, tile]
        for c in range(FRONTS):
            total = jnp.sum(arrived[r, :, c].astype(jnp.float32), axis=0)
            row = lax.broadcasted_iota(jnp.int32, (RANK, WIDTH), 0)
            rank_space = jnp.where(row < ranks[c], total, 0.0).astype(jnp.bfloat16)
            projected = lax.dot_general(
                cols_v[c], rank_space, (((0,), (0,)), ((), ())), preferred_element_type=jnp.float32
            )
            reduced = (right_v[c, :, chunk_cols(r)].astype(jnp.float32) - projected).astype(jnp.bfloat16)
            out[c, :, chunk_cols(r)] = jnp.dot(
                diag_v[c], reduced, preferred_element_type=jnp.float32
            ).astype(jnp.bfloat16)

    def sent(r):
        all_ring(r).wait_send()
        all_pair(r).wait_send()

    order = (2, 1, 3, 0)
    for r in range(CHUNKS):
        for i in range(len(pieces(r))):
            for way in (0, 1):
                wait_ring(r, i, way)
                if i + 2 < NP:
                    ring(r, i + 2, way).start()
                    if i + 3 == NP and r + 1 == CHUNKS:
                        ring(r, NP, way).start()
                elif r + 1 < CHUNKS:
                    ring(r + 1, i + 2 - NP, way).start()
                pair(r, i, way).start()
            if r == 0 and i < 3:
                pl.when(ground)(functools.partial(told, i))
            if (r, i) == (0, 6):
                pl.when(ground)(column_entered)
            if (r, i) == (1, 1):
                pl.when(ground)(all_entered)
            if (r, i) == (1, 3):
                pl.when(z > 0)(lambda: pl.semaphore_wait(row_sem.at[4], 1))
            if i == 0 and r + 1 < CHUNKS:
                pair_own(r + 1).start()
                keep_own(r + 1).start()
            if r >= 1:
                if i == 0:
                    chunk_ready(r - 1)
                after = 3 if r == 1 else 0
                if after <= i < after + NY:
                    sums(r - 1, order[i - after])
            if r >= 2 and i == 4:
                finish(r - 2)
            if r >= 1 and i == 5:
                sent(r - 1)
    last = CHUNKS - 1
    chunk_ready(last)
    for dy in order:
        sums(last, dy)
    finish(last - 1)
    sent(last)
    for r in range(CHUNKS - 1):
        all_scatter(r).wait_send()
    finish(last)
    all_scatter(last).wait_send()


def local(
    parent_solution, segment_ids, segment_counts, row_bases, column_bases, diag_inverse, child_right, tile_ranks
):
    bases = row_bases.reshape(FRONTS, SEG, NT * RANK, BLOCK)
    whole = pl.BlockSpec(memory_space=pl.ANY)
    scalars = pl.BlockSpec(memory_space=pltpu.SMEM)
    dma = pltpu.SemaphoreType.DMA
    result = pl.pallas_call(
        kernel,
        out_shape=pltpu.VMEM((FRONTS, BLOCK, RHS), jnp.bfloat16),
        in_specs=[scalars] * 3 + [whole] * 5,
        out_specs=pl.BlockSpec(memory_space=pltpu.VMEM),
        scratch_shapes=[pltpu.VMEM((NBLK + 1, BLOCK, WIDTH), jnp.bfloat16)] * CHUNKS
        + [
            pltpu.VMEM((FRONTS, SEG, NT * RANK, BLOCK), jnp.bfloat16),
            pltpu.VMEM((FRONTS, RANK, BLOCK), jnp.bfloat16),
            pltpu.VMEM((FRONTS, BLOCK, BLOCK), jnp.bfloat16),
            pltpu.VMEM((FRONTS, BLOCK, RHS), jnp.bfloat16),
            pltpu.VMEM((CHUNKS, NT, FRONTS, RANK, WIDTH), jnp.bfloat16),
            pltpu.VMEM((CHUNKS, NT, FRONTS, RANK, WIDTH), jnp.bfloat16),
            dma((CHUNKS,)),
            dma((2, NP + 1, 2)),
            dma((CHUNKS,)),
            dma((CHUNKS,)),
            dma((CHUNKS,)),
            dma((CHUNKS,)),
            dma((4,)),
            dma((CHUNKS,)),
            pltpu.SemaphoreType.REGULAR((5,)),
        ],
        compiler_params=pltpu.CompilerParams(
            collective_id=0, has_side_effects=True, vmem_limit_bytes=56 * 1024 * 1024
        ),
        cost_estimate=pl.CostEstimate(
            flops=2 * FRONTS * SEG * NT * RANK * BLOCK * RHS, bytes_accessed=12 << 20, transcendentals=0
        ),
    )(
        segment_ids[0], segment_counts[0].T, tile_ranks.reshape(FRONTS),
        parent_solution[0], bases, column_bases[0, :, 0], diag_inverse[0, :, 0], child_right[0, :, 0],
    )
    return result[None, :, None]


def solution(mesh):
    placed = (
        P("tile", "front", None, None),
        P("tile", None, None),
        P("tile", None, None),
        P("tile", "front", None, None, None, None, None),
        P("front", None, "tile", None, None),
        P("front", None, "tile", None, None),
        P("front", None, "tile", None, None),
        P("front", None, "tile"),
    )
    return jax.shard_map(
        local,
        mesh=mesh,
        in_specs=placed,
        out_specs=P("front", None, "tile", None, None),
        check_vma=False,
    )
```

```python
import functools

import jax
import jax.numpy as jnp
from jax import lax
from jax.experimental import pallas as pl
from jax.experimental.pallas import tpu as pltpu
from jax.sharding import PartitionSpec as P

MESH = pl.DeviceIdType.MESH

NZ = 8
NY = 4
NX = 4
NT = NY * NX
OWNED = 4
BLOCK = 256
RANK = 64
RHS = 512
SEG = 8
FRONTS = 2
WIDTH = 128
CHUNKS = RHS // WIDTH
NBLK = NZ * 2 * OWNED
GROUP = NX * RANK
PIECES = ((1, 0), (1, 1), (2, 0), (2, 1), (3, 0), (3, 1), (4, 0))
NP = len(PIECES)


def kernel(
    ids, counts, ranks, parent, bases, cols, diag, right_side, out,
    b0, b1, b2, b3, bases_v, cols_v, diag_v, right_v, part, arrived,
    ring_send, ring_recv, pair_send, pair_recv, tile_send, tile_recv, load_sem, own_sem, row_sem,
):
    blocks = (b0, b1, b2, b3)
    front = lax.axis_index("front")
    tile = lax.axis_index("tile")
    z, core = front // 2, front % 2
    y, x = tile // NX, tile % NX
    sibling = z * 2 + (1 - core)
    ahead = ((z + 1) % NZ) * 2 + core
    behind = ((z + NZ - 1) % NZ) * 2 + core

    def peer(k):
        return ((y + k // NX) % NY) * NX + (x + k % NX) % NX

    barrier = pltpu.get_barrier_semaphore()
    for other in (ahead, behind, sibling):
        pl.semaphore_signal(barrier, inc=1, device_id={"front": other}, device_id_type=MESH)
    along_x = (peer(1), peer(NX - 1))
    along_y = (peer(NX), peer((NY - 1) * NX))
    ground = z == 0

    @pl.when(ground)
    def _():
        for other in along_x + along_y:
            pl.semaphore_signal(barrier, inc=1, device_id={"tile": other}, device_id_type=MESH)

    pl.semaphore_wait(barrier, jnp.where(ground, 3 + 4, 3))

    def tell(step):
        for other in along_x if step == 0 else along_y:
            pl.semaphore_signal(row_sem.at[step], inc=1, device_id={"tile": other}, device_id_type=MESH)

    def told(step):
        pl.semaphore_wait(row_sem.at[step], 2)
        if step < 2:
            tell(step + 1)

    def column_entered():
        for k in range(1, NT):
            pl.semaphore_signal(row_sem.at[3], inc=1, device_id={"tile": peer(k)}, device_id_type=MESH)

    def all_entered():
        pl.semaphore_wait(row_sem.at[3], NT - 1)
        for chip in range(1, NZ):
            pl.semaphore_signal(
                row_sem.at[4], inc=1, device_id={"front": chip * 2 + core}, device_id_type=MESH
            )

    def place(chip, half):
        return pl.ds((chip * 2 + core) * OWNED + half * 2, 2)

    def chunk_cols(r):
        return pl.ds(r * WIDTH, WIDTH)

    def ring(r, i, way):
        hop, half = PIECES[i]
        half = half if way == 0 else 1 - half
        chip = (z + NZ - (hop - 1)) % NZ if way == 0 else (z + hop - 1) % NZ
        dst = blocks[r].at[place(chip, half)]
        if hop == 1:
            src = parent.at[pl.ds(half * 2, 2), :, chunk_cols(r)]
        else:
            src = dst
        return pltpu.make_async_remote_copy(
            src_ref=src, dst_ref=dst,
            send_sem=ring_send.at[r], recv_sem=ring_recv.at[r % 2, i, way],
            device_id={"front": ahead if way == 0 else behind}, device_id_type=MESH,
        )

    def ring_in(r, i, way):
        hop, half = PIECES[i]
        half = half if way == 0 else 1 - half
        chip = (z + NZ - hop) % NZ if way == 0 else (z + hop) % NZ
        return blocks[r].at[place(chip, half)]

    def wait_ring(r, i, way):
        here = ring_in(r, i, way)
        pltpu.make_async_remote_copy(
            src_ref=here, dst_ref=here,
            send_sem=ring_send.at[r], recv_sem=ring_recv.at[r % 2, i, way],
            device_id={"front": ahead}, device_id_type=MESH,
        ).wait_recv()

    def pair(r, i, way):
        here = ring_in(r, i, way)
        return pltpu.make_async_remote_copy(
            src_ref=here, dst_ref=here,
            send_sem=pair_send.at[r], recv_sem=pair_recv.at[r],
            device_id={"front": sibling}, device_id_type=MESH,
        )

    def pair_own(r):
        return pltpu.make_async_remote_copy(
            src_ref=parent.at[:, :, chunk_cols(r)],
            dst_ref=blocks[r].at[pl.ds(front * OWNED, OWNED)],
            send_sem=pair_send.at[r], recv_sem=pair_recv.at[r],
            device_id={"front": sibling}, device_id_type=MESH,
        )

    def keep_own(r):
        return pltpu.make_async_copy(
            parent.at[:, :, chunk_cols(r)], blocks[r].at[pl.ds(front * OWNED, OWNED)], own_sem.at[r]
        )

    def all_of(ref, send, recv):
        return pltpu.make_async_remote_copy(
            src_ref=ref, dst_ref=ref, send_sem=send, recv_sem=recv,
            device_id={"front": sibling}, device_id_type=MESH,
        )

    def all_ring(r):
        return all_of(blocks[r].at[pl.ds(0, 4 * NP)], ring_send.at[r], ring_recv.at[r % 2, 0, 0])

    def all_pair(r):
        return all_of(blocks[r].at[pl.ds(0, 4 * NP + OWNED)], pair_send.at[r], pair_recv.at[r])

    def all_scatter(r):
        return all_of(arrived.at[r, pl.ds(1, NT - 1)], tile_send.at[r], tile_recv.at[r])

    def scatter(r, k):
        return pltpu.make_async_remote_copy(
            src_ref=part.at[r, peer(k)], dst_ref=arrived.at[r, k],
            send_sem=tile_send.at[r], recv_sem=tile_recv.at[r],
            device_id={"tile": peer(k)}, device_id_type=MESH,
        )

    loads = [
        pltpu.make_async_copy(bases, bases_v, load_sem.at[0]),
        pltpu.make_async_copy(cols, cols_v, load_sem.at[1]),
        pltpu.make_async_copy(diag, diag_v, load_sem.at[2]),
        pltpu.make_async_copy(right_side, right_v, load_sem.at[3]),
    ]

    for i in (0, 1):
        for way in (0, 1):
            ring(0, i, way).start()
    pair_own(0).start()
    keep_own(0).start()
    for load in loads:
        load.start()
    pl.when(ground)(lambda: tell(0))
    for r in range(CHUNKS):
        blocks[r][NBLK] = jnp.zeros((BLOCK, WIDTH), jnp.bfloat16)

    def slot(c, q):
        s = c * SEG + q
        return jnp.where(q < counts[c, front], ids[front, s], NBLK)

    def sums(r, dy):
        to_y = (y + dy) % NY
        rows = pl.ds(pl.multiple_of(to_y * GROUP, GROUP), GROUP)
        for c in range(FRONTS):
            total = jnp.zeros((GROUP, WIDTH), jnp.float32)
            for q in range(SEG):
                total += jnp.dot(
                    bases_v[c, q, rows, :], blocks[r][slot(c, q)], preferred_element_type=jnp.float32
                )
            part[r, pl.ds(to_y * NX, NX), c] = total.astype(jnp.bfloat16).reshape(NX, RANK, WIDTH)
        for dx in range(NX):
            k = dy * NX + dx
            if k:
                scatter(r, k).start()

    def chunk_ready(r):
        all_pair(r).wait_recv()
        keep_own(r).wait()
        if r == 0:
            loads[0].wait()

    def finish(r):
        if r == 0:
            for load in loads[1:]:
                load.wait()
        all_scatter(r).wait_recv()
        arrived[r, 0] = part[r, tile]
        for c in range(FRONTS):
            total = jnp.sum(arrived[r, :, c].astype(jnp.float32), axis=0)
            row = lax.broadcasted_iota(jnp.int32, (RANK, WIDTH), 0)
            rank_space = jnp.where(row < ranks[c], total, 0.0).astype(jnp.bfloat16)
            projected = lax.dot_general(
                cols_v[c], rank_space, (((0,), (0,)), ((), ())), preferred_element_type=jnp.float32
            )
            reduced = (right_v[c, :, chunk_cols(r)].astype(jnp.float32) - projected).astype(jnp.bfloat16)
            out[c, :, chunk_cols(r)] = jnp.dot(
                diag_v[c], reduced, preferred_element_type=jnp.float32
            ).astype(jnp.bfloat16)

    def sent(r):
        all_ring(r).wait_send()
        all_pair(r).wait_send()

    order = (2, 1, 3, 0)
    for r in range(CHUNKS):
        for i in range(NP):
            for way in (0, 1):
                wait_ring(r, i, way)
                if i + 2 < NP:
                    ring(r, i + 2, way).start()
                elif r + 1 < CHUNKS:
                    ring(r + 1, i + 2 - NP, way).start()
                pair(r, i, way).start()
            if r == 0 and i < 3:
                pl.when(ground)(functools.partial(told, i))
            if (r, i) == (0, 6):
                pl.when(ground)(column_entered)
            if (r, i) == (1, 1):
                pl.when(ground)(all_entered)
            if (r, i) == (1, 3):
                pl.when(z > 0)(lambda: pl.semaphore_wait(row_sem.at[4], 1))
            if i == 0 and r + 1 < CHUNKS:
                pair_own(r + 1).start()
                keep_own(r + 1).start()
            if r >= 1:
                if i == 0:
                    chunk_ready(r - 1)
                after = 3 if r == 1 else 0
                if after <= i < after + NY:
                    sums(r - 1, order[i - after])
            if r >= 2 and i == 4:
                finish(r - 2)
            if r >= 1 and i == 5:
                sent(r - 1)
    last = CHUNKS - 1
    chunk_ready(last)
    for dy in order:
        sums(last, dy)
    finish(last - 1)
    sent(last)
    for r in range(CHUNKS - 1):
        all_scatter(r).wait_send()
    finish(last)
    all_scatter(last).wait_send()


def local(
    parent_solution, segment_ids, segment_counts, row_bases, column_bases, diag_inverse, child_right, tile_ranks
):
    bases = row_bases.reshape(FRONTS, SEG, NT * RANK, BLOCK)
    whole = pl.BlockSpec(memory_space=pl.ANY)
    scalars = pl.BlockSpec(memory_space=pltpu.SMEM)
    dma = pltpu.SemaphoreType.DMA
    result = pl.pallas_call(
        kernel,
        out_shape=pltpu.VMEM((FRONTS, BLOCK, RHS), jnp.bfloat16),
        in_specs=[scalars] * 3 + [whole] * 5,
        out_specs=pl.BlockSpec(memory_space=pltpu.VMEM),
        scratch_shapes=[pltpu.VMEM((NBLK + 1, BLOCK, WIDTH), jnp.bfloat16)] * CHUNKS
        + [
            pltpu.VMEM((FRONTS, SEG, NT * RANK, BLOCK), jnp.bfloat16),
            pltpu.VMEM((FRONTS, RANK, BLOCK), jnp.bfloat16),
            pltpu.VMEM((FRONTS, BLOCK, BLOCK), jnp.bfloat16),
            pltpu.VMEM((FRONTS, BLOCK, RHS), jnp.bfloat16),
            pltpu.VMEM((CHUNKS, NT, FRONTS, RANK, WIDTH), jnp.bfloat16),
            pltpu.VMEM((CHUNKS, NT, FRONTS, RANK, WIDTH), jnp.bfloat16),
            dma((CHUNKS,)),
            dma((2, NP, 2)),
            dma((CHUNKS,)),
            dma((CHUNKS,)),
            dma((CHUNKS,)),
            dma((CHUNKS,)),
            dma((4,)),
            dma((CHUNKS,)),
            pltpu.SemaphoreType.REGULAR((5,)),
        ],
        compiler_params=pltpu.CompilerParams(
            collective_id=0, has_side_effects=True, vmem_limit_bytes=56 * 1024 * 1024
        ),
        cost_estimate=pl.CostEstimate(
            flops=2 * FRONTS * SEG * NT * RANK * BLOCK * RHS, bytes_accessed=12 << 20, transcendentals=0
        ),
    )(
        segment_ids[0], segment_counts[0].T, tile_ranks.reshape(FRONTS),
        parent_solution[0], bases, column_bases[0, :, 0], diag_inverse[0, :, 0], child_right[0, :, 0],
    )
    return result[None, :, None]


def solution(mesh):
    placed = (
        P("tile", "front", None, None),
        P("tile", None, None),
        P("tile", None, None),
        P("tile", "front", None, None, None, None, None),
        P("front", None, "tile", None, None),
        P("front", None, "tile", None, None),
        P("front", None, "tile", None, None),
        P("front", None, "tile"),
    )
    return jax.shard_map(
        local,
        mesh=mesh,
        in_specs=placed,
        out_specs=P("front", None, "tile", None, None),
        check_vma=False,
    )
```
